128 devices in a mesh: bulk: 32 (over x, z, core), contact: 4 (over y).
Axes of the slice: x: 4, y: 4, z: 4, core: 2. Of those that a mesh axis runs over, the one named last changes fastest.
Arguments:
- k_inv: float32 [262144, 2048], P(('bulk', 'contact'))
- mortar_slave: float32 [32768, 256], P(('bulk', 'contact')), may hold values from -0.375 to 0.375
- mortar_master: float32 [32768, 256], P(('bulk', 'contact')), may hold values from -0.375 to 0.375
- force: float32 [262144, 256], P(('bulk', 'contact')), may hold values from -6 to 6
- lam_glue: float32 [32768, 256], P(('bulk', 'contact')), may hold values from -6 to 6
- lam_contact: float32 [32768, 256], P(('bulk', 'contact')), may hold values from 0 to 1
- master_map: int32 [128], P(('bulk', 'contact')), may hold values from 0 to 3, as said below
- on_surface: int32 [128], P(('bulk', 'contact')), may hold values 0 or 1
- step_type: int32 [2, 256], replicated, may hold values from 0 to 2
- active: int32 [2, 32768, 256], P(None, ('bulk', 'contact')), may hold values 0 or 1
- expand_len: float32 [256], replicated, may hold values from 0.05 to 0.3
Outputs:
- glue_final: float32 [32768, 256], P(('bulk', 'contact'))
- contact_final: float32 [32768, 256], P(('bulk', 'contact'))
- grad_glue_final: float32 [32768, 256], P(('bulk', 'contact'))
- grad_contact_final: float32 [32768, 256], P(('bulk', 'contact'))
The draws below stay inside these ranges and needn't reach their ends.
Inputs may be any that keep to these rules, and one draw needn't show every extreme that they name: master_map never names the subdomain's own position in its group of 4.
All inputs are finite; a program needn't handle non-finite values. No bound on the sum of `on_surface` or of `active` on one device may be relied on, other than what follows from the above.
Results may differ from the reference program's by a relative error of at most 0.0003.
Values sent between devices are 32-bit elements; how exact they have to be, the bound alone decides.
No kernel may reach another device: no remote copies, remote signals or barrier semaphores. Data moves between devices by JAX's collectives and lax.ppermute only.
A program may use at most 128 MiB of HBM per device.

```python
import math
import jax
import jax.numpy as jnp
from jax import lax

NS = 2048
FACE = 256
MORTAR = 256
LOADS = 256
ITERS = 2
GROUP = 4
SUB = 128


def draw_k_inv(key, part):

    def single(index):
        sub_key = jax.random.fold_in(key, index)
        mixing = jax.random.normal(jax.random.fold_in(sub_key, 1), (NS, NS), jnp.float32)
        diag_part = jax.random.uniform(jax.random.fold_in(sub_key, 2), (NS,), jnp.float32, 0.5, 2.0)
        gram = jnp.dot(mixing, mixing.T, precision=lax.Precision.HIGHEST) / (2.0 * NS)
        result = gram + jnp.diag(diag_part)
        return result
    whole = lax.map(single, jnp.arange(SUB, dtype=jnp.int32))
    return whole.reshape(SUB * NS, NS)


def draw_master_map(key, part):
    offset = jax.random.randint(jax.random.fold_in(key, 7), (SUB,), 1, GROUP)
    offset = offset.at[0].set(GROUP - 1).at[1].set(GROUP - 1)
    position = jnp.arange(SUB, dtype=jnp.int32) % GROUP
    return ((position + offset) % GROUP).astype(jnp.int32)


def set_ends(values, stream_key, smallest, top_value):
    extent = values.shape
    index_at = [jax.random.randint(jax.random.fold_in(stream_key, axis), (), 0, extent[axis]) for axis in range(len(extent))]
    values = values.at[tuple(index_at)].set(smallest)
    longest = extent.index(max(extent))
    index_at[longest] = (index_at[longest] + 1) % extent[longest]
    return values.at[tuple(index_at)].set(top_value)


def steps_of(key, dims, pieces, least, largest):
    level = 1.0
    for dim, shards_of in pieces:
        draws = jax.random.uniform(jax.random.fold_in(jax.random.fold_in(key, 6), dim), (shards_of,), jnp.float32, least / len(pieces), largest / len(pieces))
        level = level * jnp.repeat(jnp.exp(draws), dims[dim] // shards_of).reshape((-1,) + (1,) * (len(dims) - 1 - dim))
    return level


def centred(own_key, dims, deviation, limit, pieces=(), held_as=jnp.bfloat16):
    array = jax.random.normal(own_key, dims, jnp.float32) * deviation
    if len(pieces) > 0:
        array = steps_of(own_key, dims, pieces, -0.22, 0.18) * array
    return jnp.clip(array, min=-limit, max=limit).astype(held_as)


def setup_inputs(seed: int = 0) -> dict:
    streams_of = jax.random.split(jax.random.key(seed), 12)
    k_inv = draw_k_inv(jax.random.fold_in(streams_of[11], 71), 0)
    mortar_slave = centred(streams_of[1], (SUB * MORTAR, MORTAR), MORTAR ** -0.5, 0.375, ((0, 128),), jnp.float32)
    mortar_master = centred(streams_of[2], (SUB * MORTAR, MORTAR), MORTAR ** -0.5, 0.375, ((0, 128),), jnp.float32)
    force = centred(streams_of[3], (SUB * NS, LOADS), 1.0, 6.0, ((0, 128),), jnp.float32)
    lam_glue = centred(streams_of[4], (SUB * FACE, LOADS), 1.0, 6.0, ((0, 128),), jnp.float32)
    lam_contact = jnp.clip(1.0 * jax.random.uniform(streams_of[5], (SUB * MORTAR, LOADS), jnp.float32) ** steps_of(streams_of[5], (SUB * MORTAR, LOADS), ((0, 128),), -0.2, 0.2), 0.0, 1.0)
    master_map = draw_master_map(jax.random.fold_in(streams_of[11], 71), 0)
    on_surface = set_ends((jax.random.randint(streams_of[7], (SUB,), 0, 2) < 1).astype(jnp.int32), jax.random.fold_in(streams_of[7], 1), 0, 1)
    step_type = set_ends(jax.random.randint(streams_of[8], (ITERS, LOADS), 0, 3), jax.random.fold_in(streams_of[8], 1), 0, 2).astype(jnp.int32)
    active = set_ends((jax.random.randint(streams_of[9], (ITERS, SUB * MORTAR, LOADS), 0, 4) < 1).astype(jnp.int32), jax.random.fold_in(streams_of[9], 1), 0, 1)
    expand_len = jnp.clip(jnp.exp(jax.random.uniform(streams_of[10], (LOADS,), jnp.float32, math.log(0.05), math.log(0.3))), 0.05, 0.3)
    return {"k_inv": k_inv, "mortar_slave": mortar_slave, "mortar_master": mortar_master, "force": force, "lam_glue": lam_glue, "lam_contact": lam_contact, "master_map": master_map, "on_surface": on_surface, "step_type": step_type, "active": active, "expand_len": expand_len}


precise = lax.Precision.HIGHEST


def inner(first_glue, first_contact, second_glue, second_contact):
    return jnp.sum(first_glue * second_glue, axis=(0, 1)) + jnp.sum(first_contact * second_contact, axis=(0, 1))


def reference(k_inv, mortar_slave, mortar_master, force, lam_glue, lam_contact, master_map, on_surface, step_type, active, expand_len):
    k_blocks = k_inv.reshape(SUB, NS, NS)
    slave_blocks = mortar_slave.reshape(SUB, MORTAR, MORTAR)
    master_blocks = mortar_master.reshape(SUB, MORTAR, MORTAR)
    load = force.reshape(SUB, NS, LOADS)
    surface = on_surface.astype(jnp.float32)[:, None, None]
    glue_mask = (jnp.arange(SUB) < SUB - GROUP).astype(jnp.float32)[:, None, None]
    master_pick = (master_map.reshape(SUB // GROUP, GROUP)[:, :, None] == jnp.arange(GROUP, dtype=jnp.int32)[None, None, :]).astype(jnp.float32)
    groups = SUB // GROUP

    def operate(glue_dual, contact_dual, primal_load):
        previous = jnp.concatenate([jnp.zeros((GROUP, FACE, LOADS), jnp.float32), glue_dual[:-GROUP]], axis=0)
        slave_term = jnp.einsum('smc,smr->scr', slave_blocks, contact_dual, precision=precise) * surface
        master_term = jnp.einsum('smc,smr->scr', master_blocks, contact_dual, precision=precise) * surface
        received = jnp.einsum('bjt,bjcr->btcr', master_pick, master_term.reshape(groups, GROUP, MORTAR, LOADS), precision=precise).reshape(SUB, MORTAR, LOADS)
        interior = jnp.zeros((SUB, NS - 2 * FACE - MORTAR, LOADS), jnp.float32)
        pushed = jnp.concatenate([-previous, glue_dual, slave_term - received, interior], axis=1) - primal_load
        response = jnp.einsum('sij,sjr->sir', k_blocks, pushed, precision=precise)
        following = jnp.concatenate([response[GROUP:, :FACE], jnp.zeros((GROUP, FACE, LOADS), jnp.float32)], axis=0)
        glue_out = (response[:, FACE:2 * FACE] - following) * glue_mask
        contact_face = response[:, 2 * FACE:2 * FACE + MORTAR]
        master_face = jnp.einsum('bjt,btcr->bjcr', master_pick, contact_face.reshape(groups, GROUP, MORTAR, LOADS), precision=precise).reshape(SUB, MORTAR, LOADS)
        own_gap = jnp.einsum('smc,scr->smr', slave_blocks, contact_face, precision=precise)
        other_gap = jnp.einsum('smc,scr->smr', master_blocks, master_face, precision=precise)
        return glue_out, (own_gap - other_gap) * surface

    glue_now = lam_glue.reshape(SUB, FACE, LOADS) * glue_mask
    contact_now = lam_contact.reshape(SUB, MORTAR, LOADS)
    grad_glue, grad_contact = operate(glue_now, contact_now, load)
    prev_glue = jnp.zeros_like(glue_now)
    prev_contact = jnp.zeros_like(contact_now)
    prev_image_glue = jnp.zeros_like(glue_now)
    prev_image_contact = jnp.zeros_like(contact_now)
    curvature = jnp.ones((LOADS,), jnp.float32)
    for sweep in range(ITERS):
        active_now = active[sweep].reshape(SUB, MORTAR, LOADS).astype(jnp.float32)
        kinds = step_type[sweep]
        is_cg = (kinds == 0).astype(jnp.float32)
        is_expand = (kinds == 1).astype(jnp.float32)
        is_chop = (kinds == 2).astype(jnp.float32)
        free_glue = grad_glue
        free_contact = grad_contact * (1.0 - active_now) * surface
        chopped = jnp.minimum(grad_contact, 0.0) * active_now * surface
        if sweep > 0:
            conj_ratio = inner(free_glue, free_contact, prev_image_glue, prev_image_contact) / curvature
        else:
            conj_ratio = jnp.zeros((LOADS,), jnp.float32)
        keep = is_cg + is_expand
        dir_glue = keep * free_glue - is_cg * conj_ratio * prev_glue
        dir_contact = keep * free_contact - is_cg * conj_ratio * prev_contact + is_chop * chopped
        image_glue, image_contact = operate(dir_glue, dir_contact, 0.0)
        descent = inner(grad_glue, grad_contact, dir_glue, dir_contact)
        curvature = inner(dir_glue, dir_contact, image_glue, image_contact)
        step_len = jnp.where(kinds == 1, expand_len, descent / curvature)
        half_glue = glue_now - step_len * dir_glue
        half_contact = contact_now - step_len * dir_contact
        correction = is_expand * surface * jnp.maximum(-half_contact, 0.0)
        fix_glue, fix_contact = operate(jnp.zeros_like(half_glue), correction, 0.0)
        glue_now = half_glue
        contact_now = half_contact + correction
        grad_glue = grad_glue - step_len * image_glue + fix_glue
        grad_contact = grad_contact - step_len * image_contact + fix_contact
        prev_glue, prev_contact = dir_glue, dir_contact
        prev_image_glue, prev_image_contact = image_glue, image_contact
    return (glue_now.reshape(SUB * FACE, LOADS), contact_now.reshape(SUB * MORTAR, LOADS),
            grad_glue.reshape(SUB * FACE, LOADS), grad_contact.reshape(SUB * MORTAR, LOADS))
```

```python
import jax
import jax.numpy as jnp
from jax import lax
from jax.sharding import PartitionSpec as P

three_pass = lax.Precision.HIGH
everyone = ("bulk", "contact")


def mul(left, right):
    return jnp.dot(left, right, precision=three_pass)


def mul_t(left, right):
    return lax.dot_general(left, right, (((0,), (0,)), ((), ())), precision=three_pass)


def along_bulk(value, steps):
    count = lax.axis_size("bulk")
    leading, last = (max(0, -steps), min(count, count - steps))
    return lax.ppermute(value, "bulk", [(s, s + steps) for s in range(leading, last)])


def from_block(value, offset):
    count = lax.axis_size("contact")
    return lax.ppermute(value, "contact", [((d + offset) % count, d) for d in range(count)])


def total(rows):
    k, n = rows.shape
    count = lax.axis_size("bulk") * lax.axis_size("contact")
    spread = jnp.broadcast_to(rows.reshape(1, k * n), (count, k * n))
    got = lax.all_to_all(spread, everyone, 0, 0, tiled=True)
    return jnp.sum(got, axis=0).reshape(k, n)


def col(value):
    return jnp.sum(value, axis=0, keepdims=True)


def per_device(
    k_inv,
    mortar_slave,
    mortar_master,
    force,
    lam_glue,
    lam_contact,
    master_map,
    on_surface,
    step_type,
    active,
    expand_len,
):
    f = lam_glue.shape[0]
    m = lam_contact.shape[0]
    n = lam_glue.shape[1]
    rows = 2 * f + m
    bulk_at = lax.axis_index("bulk")
    own_mask = (bulk_at < lax.axis_size("bulk") - 1).astype(jnp.float32)
    prev_mask = (bulk_at > 0).astype(jnp.float32)
    here = lax.axis_index("contact").astype(jnp.float32)
    surface = on_surface[0].astype(jnp.float32)
    slave = mortar_slave * surface
    master = mortar_master * surface
    note = jnp.broadcast_to(master_map[0].astype(jnp.float32), (8, n))
    active_f = active.astype(jnp.float32)

    first = jnp.concatenate([master, lam_contact, note], axis=0)
    first_r = from_block(first, 1)
    first_l = from_block(first, 3)
    far_master = from_block(first_l[:m], 3)
    far_lam = from_block(first_r[m:], 1)
    second = jnp.concatenate([slave, active_f[0]], axis=0)
    second, far_master, far_lam = lax.optimization_barrier((second, far_master, far_lam))
    second_r = from_block(second, 1)
    second_l = from_block(second, 3)
    far_slave = from_block(second_l[:m], 3)
    far_active = from_block(second_r[m:], 1)

    masters = jnp.concatenate([first_r[:m], far_master, first_l[:m]], axis=0)
    lam_c = jnp.concatenate([lam_contact, first_r[m : 2 * m], far_lam[:m], first_l[m : 2 * m]], axis=0)
    names = [
        (note_o == here).astype(jnp.float32)
        for note_o in (first_r[2 * m, 0], far_lam[m, 0], first_l[2 * m, 0])
    ]
    own_master = master_map[0].astype(jnp.float32)
    picks = [
        (own_master == (lax.axis_index("contact") + o) % lax.axis_size("contact")).astype(jnp.float32)
        for o in (1, 2, 3)
    ]
    masters_named = jnp.concatenate(
        [masters[o * m : (o + 1) * m] * names[o] for o in range(3)], axis=0
    )
    slaves = [slave, second_r[:m], far_slave, second_l[:m]]
    act0 = jnp.concatenate([active_f[0], second_r[m:], far_active, second_l[m:]], axis=0)
    block_surface = jnp.concatenate(
        [jnp.broadcast_to(surface, (m, 1)), jnp.ones((3 * m, 1), jnp.float32)], axis=0
    )

    k_top = k_inv[:rows]
    k_small = k_top[:, :rows]
    base = mul(k_top, force)

    def push(contact):
        return mul_t(slave, contact[:m]) - mul_t(masters_named, contact[m:])

    def assemble(glue, contact):
        return jnp.concatenate([-glue[f:], glue[:f], push(contact)], axis=0)

    def glue_trade(y):
        return along_bulk(y[f : 2 * f], 1), along_bulk(y[:f], -1)

    def group(y):
        return [from_block(y, 1), from_block(y, 3), from_block(y, 2)]

    def gaps(y, traded, others):
        before, after = traded
        glue = jnp.concatenate(
            [(y[f : 2 * f] - after) * own_mask, (before - y[:f]) * prev_mask], axis=0
        )
        own = y[2 * f :]
        blocks = [others[0], others[2], others[1]]
        chosen = picks[0] * blocks[0] + picks[1] * blocks[1] + picks[2] * blocks[2]
        below = mul(masters, own)
        contact = jnp.concatenate(
            [mul(slave, own) - mul(master, chosen)]
            + [mul(slaves[o + 1], blocks[o]) - below[o * m : (o + 1) * m] for o in range(3)],
            axis=0,
        )
        return glue, contact

    expand = expand_len[None, :]
    kinds = [step_type[i][None, :] for i in range(2)]
    is_cg = [(t == 0).astype(jnp.float32) for t in kinds]
    is_expand = [(t == 1).astype(jnp.float32) for t in kinds]
    is_chop = [(t == 2).astype(jnp.float32) for t in kinds]

    lam_g = lam_glue * own_mask
    lam_prev = along_bulk(lam_g, 1)
    y = mul(k_small, assemble(jnp.concatenate([lam_g, lam_prev], axis=0), lam_c)) - base
    others = group(y[2 * f :])
    traded = glue_trade(y)
    grad_g, grad_c = gaps(y, traded, others)

    keep = is_cg[0] + is_expand[0]
    dir_g = keep * grad_g
    dir_c = keep * grad_c * (1.0 - act0) + is_chop[0] * jnp.minimum(grad_c, 0.0) * act0
    fix0 = is_expand[0] * jnp.maximum(expand * dir_c - lam_c, 0.0) * block_surface
    w_dir = assemble(dir_g, dir_c)
    y_dir = mul(k_small, w_dir)
    y_fix = mul(k_small[:, 2 * f :], push(fix0))
    y_sent = jnp.where(kinds[0] == 1, expand * y_dir - y_fix, y_dir)
    sums = jnp.concatenate(
        [
            col(w_dir * y_dir),
            col(grad_g[:f] * dir_g[:f]) + col(grad_c[:m] * dir_c[:m]),
            col(w_dir * y_fix),
        ],
        axis=0,
    )
    both = group(jnp.concatenate([y_sent[2 * f :], active_f[1]], axis=0))
    traded = glue_trade(y_sent)
    sums = total(sums)
    curv0, desc0, cross0 = sums[0:1], sums[1:2], sums[2:3]
    others = [v[:m] for v in both]
    act1 = jnp.concatenate([active_f[1], both[0][m:], both[2][m:], both[1][m:]], axis=0)
    step0 = jnp.where(kinds[0] == 1, expand, desc0 / curv0)
    scale0 = jnp.where(kinds[0] == 1, 1.0, step0)
    image_g, image_c = gaps(y_sent, traded, others)
    grad_g = grad_g - scale0 * image_g
    grad_c = grad_c - scale0 * image_c
    lam1_g = lam_g - step0 * dir_g[:f]
    lam1_c = lam_c - step0 * dir_c + fix0

    keep = is_cg[1] + is_expand[1]
    free_g = keep * grad_g
    free_c = keep * grad_c * (1.0 - act1) + is_chop[1] * jnp.minimum(grad_c, 0.0) * act1
    fix1 = is_expand[1] * jnp.maximum(expand * free_c - lam1_c, 0.0) * block_surface
    long1 = jnp.where(kinds[1] == 1, expand, 1.0)
    w_now = assemble(long1 * free_g, long1 * free_c - fix1)
    y_now = mul(k_small, w_now)
    first_sum = col(w_now * y_dir)
    sums = jnp.concatenate(
        [
            first_sum,
            first_sum + col(w_dir * y_now),
            col(w_now * y_now),
            col(grad_g[:f] * free_g[:f]) + col(grad_c[:m] * free_c[:m]),
        ],
        axis=0,
    )
    faces = jnp.concatenate([y_now[2 * f :], y_dir[2 * f :]], axis=0)
    others = group(faces)
    after = along_bulk(jnp.concatenate([y_now[:f], y_dir[:f]], axis=0), -1)
    sums = total(sums)
    left_over = desc0 - step0 * curv0 + is_expand[0] * cross0
    conj = is_cg[1] * sums[0:1] / curv0
    curv1 = sums[2:3] - conj * sums[1:2] + conj * conj * curv0
    desc1 = sums[3:4] - conj * left_over
    step1 = jnp.where(kinds[1] == 1, expand, desc1 / curv1)
    scale1 = jnp.where(kinds[1] == 1, 1.0, step1)

    chosen = picks[0] * others[0] + picks[1] * others[2] + picks[2] * others[1]
    glue_image = (
        (y_now[f : 2 * f] - conj * y_dir[f : 2 * f]) - (after[:f] - conj * after[f:])
    ) * own_mask
    contact_image = mul(slave, y_now[2 * f :] - conj * y_dir[2 * f :]) - mul(
        master, chosen[:m] - conj * chosen[m:]
    )
    glue_out = lam1_g - step1 * (free_g[:f] - conj * dir_g[:f])
    contact_out = lam1_c[:m] - step1 * (free_c[:m] - conj * dir_c[:m]) + fix1[:m]
    return (
        glue_out,
        contact_out,
        grad_g[:f] - scale1 * glue_image,
        grad_c[:m] - scale1 * contact_image,
    )


def solution(mesh):
    whole = P(("bulk", "contact"), None)
    flat = P(("bulk", "contact"))
    return jax.shard_map(
        per_device,
        mesh=mesh,
        in_specs=(
            whole, whole, whole, whole, whole, whole, flat, flat,
            P(), P(None, ("bulk", "contact"), None), P(),
        ),
        out_specs=(whole, whole, whole, whole),
        check_vma=False,
    )
```

```python
import functools

import jax
import jax.numpy as jnp
from jax import lax
from jax.experimental import pallas as pl
from jax.experimental.pallas import tpu as pltpu
from jax.sharding import PartitionSpec as P

everyone = ("bulk", "contact")
f32, bf16 = jnp.float32, jnp.bfloat16
small_vmem, large_vmem = 12 * 1024 * 1024, 60 * 1024 * 1024
NOTE = 8


def along_bulk(value, steps):
    count = lax.axis_size("bulk")
    leading, last = (max(0, -steps), min(count, count - steps))
    return lax.ppermute(value, "bulk", [(s, s + steps) for s in range(leading, last)])


def trade(value, start):
    count = lax.axis_size("bulk")
    pairs = [(s, s + 1) for s in range(start, count - 1, 2)]
    return lax.ppermute(value, "bulk", pairs + [(b, a) for a, b in pairs])


def from_block(value, offset):
    count = lax.axis_size("contact")
    return lax.ppermute(value, "contact", [((d + offset) % count, d) for d in range(count)])


def everywhere(spread):
    return lax.all_to_all(spread, everyone, 0, 0, tiled=True)


def split(value):
    high = value.astype(bf16)
    return high, (value - high.astype(f32)).astype(bf16)


def mul(left, right, contract=1):
    def one(a, b):
        return lax.dot_general(a, b, (((contract,), (0,)), ((), ())), preferred_element_type=f32)

    return one(left[0], right[0]) + (one(left[0], right[1]) + one(left[1], right[0]))


def col(value):
    return jnp.sum(value, axis=0, keepdims=True)


def place():
    bulk_at = lax.axis_index("bulk")
    own = (bulk_at < lax.axis_size("bulk") - 1).astype(f32)
    prev = (bulk_at > 0).astype(f32)
    return bulk_at % 2 == 0, own, prev


def named(notes):
    here = lax.axis_index("contact").astype(f32)
    return [jnp.where(note[0:1] == here, note[1:2], 0.0) for note in notes]


def push(slave, masters, own, others):
    out = mul(slave, split(own), 0)
    for block, dual in zip(masters, others):
        out = out - mul(block, split(dual), 0)
    return out


def chosen(master_map, blocks):
    count = lax.axis_size("contact")
    offset = lax.rem(master_map[0] - lax.axis_index("contact") + count, count)
    return jnp.where(offset == 1, blocks[0], jnp.where(offset == 2, blocks[1], blocks[2]))


def spread_sums(out, rows):
    n = rows[0].shape[1] // 2
    tile = jnp.concatenate([row[:, i * n : (i + 1) * n] for row in rows for i in range(2)], axis=0)
    out[...] = jnp.broadcast_to(tile[None], out.shape)


def gather_sums(got, k):
    tile = jnp.sum(got[...], axis=0)
    return [jnp.concatenate([tile[2 * i : 2 * i + 1], tile[2 * i + 1 : 2 * i + 2]], axis=1) for i in range(k)]


def kinds_of(step_type, at):
    kind = step_type[at : at + 1]
    return kind == 1, (kind == 0).astype(f32), (kind == 1).astype(f32), (kind == 2).astype(f32)


def direction(kinds, glue, contact, active):
    _, is_cg, is_expand, is_chop = kinds
    keep = is_cg + is_expand
    return (
        [keep * g for g in glue],
        [
            keep * g * (1.0 - a) + is_chop * jnp.minimum(g, 0.0) * a
            for g, a in zip(contact, active)
        ],
    )


def correction(kinds, expand, lam, contact, surfaces):
    return [
        kinds[2] * s * jnp.maximum(expand * d - v, 0.0) for v, d, s in zip(lam, contact, surfaces)
    ]


def base_kernel(k_ref, force_ref, base_ref, high_ref, low_ref):
    step = pl.program_id(0)
    high, low = split(k_ref[...])
    part = mul((high, low), split(force_ref[...]))

    @pl.when(step == 0)
    def _():
        base_ref[...] = part

    @pl.when(step > 0)
    def _():
        base_ref[...] += part

    @pl.when(step < 3)
    def _():
        high_ref[...] = high
        low_ref[...] = low


def prepare_kernel(
    master, lam, slave, active, master_map, on_surface, first_out, second_out, later_out
):
    m, n = lam.shape
    row = lax.broadcasted_iota(jnp.int32, (NOTE, n), 0)
    first_out[2 * m :] = jnp.where(
        row == 0, master_map[0], jnp.where(row == 1, on_surface[0], 0)
    ).astype(f32)
    first_out[:m] = master[...]
    first_out[m : 2 * m] = lam[...]
    first_out.send()
    second_out[:m] = slave[...]
    second_out[m:] = active[0].astype(f32)
    second_out.send()
    later_out[...] = active[1].astype(f32)


def send_faces(y, first_out, second_out, f):
    even, _, _ = place()
    first_out[...] = jnp.where(even, y[f : 2 * f], y[:f])
    second_out[...] = jnp.where(even, y[:f], y[f : 2 * f])
    first_out.send()
    second_out.send()


def glue_gaps(left, right, first_got, second_got):
    even, own, prev = place()
    after = jnp.where(even, first_got, second_got)
    before = jnp.where(even, second_got, first_got)
    return [(right - after) * own, (before - left) * prev]


def faces_of(first_sent, second_sent):
    even, _, _ = place()
    return jnp.where(even, second_sent, first_sent), jnp.where(even, first_sent, second_sent)


def contact_gaps(slaves, masters, own, blocks, master_map, surfaces):
    own_s = split(own)
    block_s = [split(v) for v in blocks]
    picked = tuple(chosen(master_map, [v[i] for v in block_s]) for i in range(2))
    out = [surfaces[0] * (mul(slaves[0], own_s) - mul(masters[0], picked))]
    for o in range(3):
        out.append(surfaces[o + 1] * (mul(slaves[o + 1], block_s[o]) - mul(masters[o + 1], own_s)))
    return out


def unpack(first, first_r, first_l, m_far, note_far):
    m = m_far.shape[0]
    top, rest = pl.ds(0, m), pl.ds(m, m + NOTE)
    masters = (first.part(top), first_r.part(top), m_far, first_l.part(top))
    notes = (first.part(rest), first_r.part(rest), note_far, first_l.part(rest))
    return masters, notes


def start_kernel(
    slave, first, first_r, first_l, m_far, note_far, lam_glue, lam_prev, high, low, base,
    on_surface, first_out, second_out, contact_out,
):
    f = lam_glue.shape[0]
    m = slave.shape[0]
    _, own, _ = place()
    surface = on_surface[0].astype(f32)
    masters, notes = unpack(first, first_r, first_l, m_far, note_far)
    duals = [v[:m] * name for v, name in zip(notes[1:], named([v[m:] for v in notes[1:]]))]
    contact = push(split(slave[...]), blocks_of(masters[1:]), notes[0][:m] * surface, duals)
    w = jnp.concatenate([-lam_prev[...], lam_glue[...] * own, contact], axis=0)
    y = mul((high[...], low[...]), split(w)) - base[...]
    send_faces(y, first_out, second_out, f)
    contact_out[...] = y[2 * f :]


def blocks_of(refs):
    return [split(v[...]) for v in refs]


def first_kernel(
    first_sent, second_sent, contact_sent, first_got, second_got, c1, c2, c3,
    second, second_r, second_l, s_far, a_far, first, first_r, first_l, m_far, note_far,
    step_type, expand_len, high, low, master_map,
    sums_out, first_out, second_out, contact_out, glue_state, contact_state, w_state, y_state, face_out,
):
    f = first_sent.shape[0]
    m = s_far.shape[0]
    mortar, all_notes = unpack(first, first_r, first_l, m_far, note_far)
    top, rest = pl.ds(0, m), pl.ds(m, m)
    slave_refs = (second.part(top), second_r.part(top), s_far, second_l.part(top))
    act_refs = (second.part(rest), second_r.part(rest), a_far, second_l.part(rest))
    surfaces = [v[m:][1:2] for v in all_notes]
    names = named([v[m:] for v in all_notes[1:]])
    slaves, masters = blocks_of(slave_refs), blocks_of(mortar)
    left, right = faces_of(first_sent[...], second_sent[...])
    glue = glue_gaps(left, right, first_got[...], second_got[...])
    contact = contact_gaps(
        slaves, masters, contact_sent[...], [c1[...], c2[...], c3[...]], master_map, surfaces
    )
    for at, g in enumerate(glue):
        glue_state[at * f : (at + 1) * f] = g
    for at, g in enumerate(contact):
        contact_state[at * m : (at + 1) * m] = g
    glue_state.send()
    contact_state.send()

    kinds = kinds_of(step_type, 0)
    expand = expand_len[...]
    dir_g, dir_c = direction(kinds, glue, contact, [v[...] for v in act_refs])
    fix = correction(kinds, expand, [v[:m] for v in all_notes], dir_c, surfaces)

    w = jnp.concatenate(
        [-dir_g[1], dir_g[0], push(slaves[0], masters[1:], dir_c[0], [d * b for d, b in zip(dir_c[1:], names)])],
        axis=0,
    )
    w_fix = push(slaves[0], masters[1:], fix[0], [d * b for d, b in zip(fix[1:], names)])
    y = mul((high[...], low[...]), split(w))
    y_fix = mul((high[:, 2 * f :], low[:, 2 * f :]), split(w_fix))
    sent = jnp.where(kinds[0], expand * y - y_fix, y)
    send_faces(sent, first_out, second_out, f)
    contact_out[...] = sent[2 * f :]
    contact_out.send()
    face_out[...] = y[2 * f :]
    face_out.send()
    w_state[...] = w
    y_state[...] = y
    w_state.send()
    y_state.send()
    zero = jnp.zeros_like(expand)
    spread_sums(
        sums_out,
        [col(w * y), col(glue[0] * dir_g[0]) + col(contact[0] * dir_c[0]), col(w * y_fix), zero],
    )


def second_kernel(
    first_sent, second_sent, contact_sent, first_got, second_got, c1, c2, c3,
    second, second_r, second_l, s_far, a_far, first, first_r, first_l, m_far, note_far,
    step_type, expand_len, got, glue_state, contact_state, lam_glue,
    l0, l_r, l_far, l_l, high, low, y_state, w_state, master_map,
    sums_out, left_out, contact_out, right_out, own_out, rows_out,
):
    f = first_sent.shape[0]
    m = s_far.shape[0]
    _, own, _ = place()
    mortar, all_notes = unpack(first, first_r, first_l, m_far, note_far)
    top, rest = pl.ds(0, m), pl.ds(m, m)
    slave_refs = (second.part(top), second_r.part(top), s_far, second_l.part(top))
    act_refs = (second.part(rest), second_r.part(rest), a_far, second_l.part(rest))
    surfaces = [v[m:][1:2] for v in all_notes]
    names = named([v[m:] for v in all_notes[1:]])
    slaves, masters = blocks_of(slave_refs), blocks_of(mortar)
    left, right = faces_of(first_sent[...], second_sent[...])
    image_g = glue_gaps(left, right, first_got[...], second_got[...])
    image_c = contact_gaps(
        slaves, masters, contact_sent[...], [c1[...], c2[...], c3[...]], master_map, surfaces
    )

    kinds = kinds_of(step_type, 0)
    expand = expand_len[...]
    curv0, desc0, cross0 = gather_sums(got, 3)
    step = jnp.where(kinds[0], expand, desc0 / curv0)
    scale = jnp.where(kinds[0], 1.0, step)
    glue = [glue_state[at * f : (at + 1) * f] for at in range(2)]
    contact = [contact_state[at * m : (at + 1) * m] for at in range(4)]
    lam_c = [v[:m] for v in all_notes]
    dir_g, dir_c = direction(kinds, glue, contact, [v[...] for v in act_refs])
    fix = correction(kinds, expand, lam_c, dir_c, surfaces)
    lam_c = [v - step * d + x for v, d, x in zip(lam_c, dir_c, fix)]
    own_out[0] = lam_glue[...] * own - step * dir_g[0]
    glue = [g - scale * x for g, x in zip(glue, image_g)]
    contact = [g - scale * x for g, x in zip(contact, image_c)]

    kinds = kinds_of(step_type, 1)
    free_g, free_c = direction(
        kinds, glue, contact,
        [l0[...], l_r[...], l_far[...], l_l[...]],
    )
    fix = correction(kinds, expand, lam_c, free_c, surfaces)
    length = jnp.where(kinds[0], expand, 1.0)
    dual = [length * d - x for d, x in zip(free_c, fix)]
    w = jnp.concatenate(
        [
            -length * free_g[1],
            length * free_g[0],
            push(slaves[0], masters[1:], dual[0], [d * b for d, b in zip(dual[1:], names)]),
        ],
        axis=0,
    )
    y = mul((high[...], low[...]), split(w))
    w_dir, y_dir = w_state[...], y_state[...]
    left_out[:f] = y[:f]
    left_out[f:] = y_dir[:f]
    right_out[:f] = y[f : 2 * f]
    right_out[f:] = y_dir[f : 2 * f]
    contact_out[...] = y[2 * f :]
    for out in (left_out, right_out, contact_out):
        out.send()
    own_out[1] = lam_c[0] + fix[0]
    own_out[2] = glue[0]
    own_out[3] = contact[0]
    own_out[4] = free_g[0]
    own_out[5] = free_c[0]
    own_out[6] = dir_g[0]
    own_out[7] = dir_c[0]
    own_out.send()
    first = col(w * y_dir)
    spread_sums(
        sums_out,
        [
            first,
            first + col(w_dir * y),
            col(w * y),
            col(glue[0] * free_g[0]) + col(contact[0] * free_c[0]),
        ],
    )
    left_over = desc0 - step * curv0 + kinds_of(step_type, 0)[2] * cross0
    rows_out[...] = jnp.concatenate([curv0, left_over] + [curv0] * 6, axis=0)


def last_kernel(
    got, rows, own_in, right, contact_sent, face_sent, after, c1, c2, c3, d1, d2, d3, slave, master, step_type,
    expand_len, master_map, on_surface, lam_g, lam_c, grad_g, grad_c,
):
    m = slave.shape[0]
    f = after.shape[0] // 2
    _, own, _ = place()
    surface = on_surface[0].astype(f32)
    kinds = kinds_of(step_type, 1)
    expand = expand_len[...]
    first, cross, curv, desc = gather_sums(got, 4)
    curv0, left_over = rows[0:1], rows[1:2]
    conj = jnp.where(step_type[1:2] == 0, first / curv0, 0.0)
    curv = curv - conj * cross + conj * conj * curv0
    desc = desc - conj * left_over
    step = jnp.where(kinds[0], expand, desc / curv)
    scale = jnp.where(kinds[0], 1.0, step)
    image_g = own * ((right[:f] - conj * right[f:]) - (after[:f] - conj * after[f:]))
    picked = chosen(master_map, [v[...] for v in (c1, c2, c3)]) - conj * chosen(
        master_map, [d1[...], d2[...], d3[...]]
    )
    image_c = surface * (
        mul(split(slave[...]), split(contact_sent[...] - conj * face_sent[...]))
        - mul(split(master[...]), split(picked))
    )
    lam_g[...] = own_in[0] - step * (own_in[4] - conj * own_in[6])
    lam_c[...] = own_in[1] - step * (own_in[5] - conj * own_in[7])
    grad_g[...] = own_in[2] - scale * image_g
    grad_c[...] = own_in[3] - scale * image_c


class Part:
    def __init__(self, whole, index):
        self.whole, self.index = whole, index

    @property
    def shape(self):
        return self.whole.ref.at[self.index].shape

    def __getitem__(self, index):
        return self.whole.arrived().at[self.index][index]


class Operand:
    def __init__(self, source, ref, sem):
        self.ref, self.here = ref, False
        self.copy = pltpu.make_async_copy(source, ref, sem)
        self.copy.start()

    @property
    def shape(self):
        return self.ref.shape

    @property
    def at(self):
        return self

    def arrived(self):
        if not self.here:
            self.copy.wait()
            self.here = True
        return self.ref

    def __getitem__(self, index):
        return self.arrived()[index]

    def part(self, index):
        return Part(self, index)


class Result:
    def __init__(self, target, ref, sem):
        self.ref, self.sent = ref, False
        self.copy = pltpu.make_async_copy(ref, target, sem)

    @property
    def shape(self):
        return self.ref.shape

    def __setitem__(self, index, value):
        self.ref[index] = value

    def send(self):
        if not self.sent:
            self.copy.start()
            self.sent = True


class Held(Operand):
    def __init__(self, ref):
        self.ref, self.here = ref, True


def call(kernel, operands, shapes, scalars=(), near=False):
    arrays = [] if near else [at for at in range(len(operands)) if at not in scalars]
    n_in, n_out = len(operands), len(shapes)

    def body(*refs):
        given, results, scratch = refs[:n_in], refs[n_in : n_in + n_out], refs[n_in + n_out :]
        sems_in, sems_out = scratch[-2:]
        ins = [v if at in scalars else Held(v) for at, v in enumerate(given)]
        for slot, at in enumerate(arrays):
            ins[at] = Operand(given[at], scratch[slot], sems_in.at[slot])
        outs = [
            Result(results[at], scratch[len(arrays) + at], sems_out.at[at]) for at in range(n_out)
        ]
        kernel(*ins, *outs)
        for at in arrays:
            ins[at].arrived()
        for out in outs:
            out.send()
        for out in outs:
            out.copy.wait()

    return pl.pallas_call(
        body,
        out_shape=[jax.ShapeDtypeStruct(s, f32) for s in shapes],
        in_specs=[
            pl.BlockSpec(
                memory_space=pltpu.SMEM if at in scalars else pltpu.VMEM if near else pltpu.HBM
            )
            for at in range(n_in)
        ],
        out_specs=[pl.BlockSpec(memory_space=pltpu.HBM) for _ in shapes],
        scratch_shapes=[pltpu.VMEM(operands[at].shape, operands[at].dtype) for at in arrays]
        + [pltpu.VMEM(s, f32) for s in shapes]
        + [pltpu.SemaphoreType.DMA((max(1, len(arrays)),)), pltpu.SemaphoreType.DMA((n_out,))],
        compiler_params=pltpu.CompilerParams(vmem_limit_bytes=small_vmem if near else large_vmem),
        name=kernel.__name__,
    )(*operands)


def per_device(
    k_inv, mortar_slave, mortar_master, force, lam_glue, lam_contact, master_map, on_surface,
    step_type, active, expand_len,
):
    f, n = lam_glue.shape
    m = lam_contact.shape[0]
    rows = 2 * f + m
    order = k_inv.shape[0]
    block = order // 8
    count = lax.axis_size("bulk") * lax.axis_size("contact")
    face, sums = (f, n), (count, 8, n // 2)
    expand = expand_len[None]

    first, second, later = call(
        prepare_kernel,
        (mortar_master, lam_contact, mortar_slave, active, master_map, on_surface),
        [(2 * m + NOTE, n), (2 * m, n), (m, n)],
        (4, 5),
    )
    first_r, first_l = from_block(first, 1), from_block(first, 3)
    second_r, second_l = from_block(second, 1), from_block(second, 3)
    lam_prev = along_bulk(lam_glue, 1)
    base, high, low = pl.pallas_call(
        base_kernel,
        grid=(8,),
        in_specs=[
            pl.BlockSpec((rows, block), lambda j: (0, j)),
            pl.BlockSpec((block, n), lambda j: (j, 0)),
        ],
        out_specs=[
            pl.BlockSpec((rows, n), lambda j: (0, 0)),
            pl.BlockSpec((rows, block), lambda j: (0, jnp.minimum(j, 2))),
            pl.BlockSpec((rows, block), lambda j: (0, jnp.minimum(j, 2))),
        ],
        out_shape=[
            jax.ShapeDtypeStruct((rows, n), f32),
            jax.ShapeDtypeStruct((rows, rows), bf16),
            jax.ShapeDtypeStruct((rows, rows), bf16),
        ],
        compiler_params=pltpu.CompilerParams(vmem_limit_bytes=small_vmem),
        cost_estimate=pl.CostEstimate(
            flops=12 * rows * order * n, bytes_accessed=4 * order * (rows + n), transcendentals=0
        ),
        name="base_kernel",
    )(k_inv, force)
    first_r, first_l, base = lax.optimization_barrier((first_r, first_l, base))
    m_far, note_far = from_block(first_l[:m], 3), from_block(first_r[m:], 1)
    s_far, a_far = from_block(second_l[:m], 3), from_block(second_r[m:], 1)
    firsts = (first, first_r, first_l, m_far, note_far)
    seconds = (second, second_r, second_l, s_far, a_far)

    def group(value):
        right, left, across = (from_block(value, o) for o in (1, 3, 2))
        return right, across, left

    def exchange(first, second, contact):
        got = trade(first, 0), trade(second, 1)
        return got + group(contact)

    one, two, contact = call(
        start_kernel,
        (mortar_slave, *firsts, lam_glue, lam_prev, high, low, base, on_surface),
        [face, face, (m, n)],
        (11,),
        near=True,
    )
    got = exchange(one, two, contact)
    later, held = lax.optimization_barrier((later, got[1]))
    got = (got[0], held) + got[2:]
    laters = (later,) + group(later)
    spread, one, two, contact, glue_state, contact_state, w_state, y_state, face_dir = call(
        first_kernel,
        (one, two, contact, *got, *seconds, *firsts, step_type, expand, high, low, master_map),
        [sums, face, face, (m, n), (2 * f, n), (4 * m, n), (rows, n), (rows, n), (m, n)],
        (22,),
        near=True,
    )
    one, two, contact, spread, laters = lax.optimization_barrier((one, two, contact, spread, laters))
    got = exchange(one, two, contact)
    spread, got = lax.optimization_barrier((spread, got))
    totals = everywhere(spread)
    face_dir, got = lax.optimization_barrier((face_dir, got))
    dirs = group(face_dir)
    spread, left, contact, right, own, kept = call(
        second_kernel,
        (one, two, contact, *got, *seconds, *firsts, step_type, expand, totals, glue_state,
         contact_state, lam_glue, *laters, high, low, y_state, w_state, master_map),
        [sums, (2 * f, n), (m, n), (2 * f, n), (8, f, n), (8, n)],
        (32,),
    )
    left, contact, spread, dirs = lax.optimization_barrier((left, contact, spread, dirs))
    after = along_bulk(left, -1)
    others = group(contact)
    totals = everywhere(spread)
    return tuple(
        call(
            last_kernel,
            (totals, kept, own, right, contact, face_dir, after, *others, *dirs,
             mortar_slave, mortar_master, step_type, expand, master_map, on_surface),
            [face, (m, n), face, (m, n)],
            (17, 18),
        )
    )


def solution(mesh):
    whole = P(("bulk", "contact"), None)
    flat = P(("bulk", "contact"))
    return jax.shard_map(
        per_device,
        mesh=mesh,
        in_specs=(
            whole, whole, whole, whole, whole, whole, flat, flat,
            P(), P(None, ("bulk", "contact"), None), P(),
        ),
        out_specs=(whole, whole, whole, whole),
        check_vma=False,
    )
```

```python
import functools

import jax
import jax.numpy as jnp
from jax import lax
from jax.experimental import pallas as pl
from jax.experimental.pallas import tpu as pltpu
from jax.sharding import PartitionSpec as P

everyone = ("bulk", "contact")
f32, bf16 = jnp.float32, jnp.bfloat16
small_vmem, middle_vmem, large_vmem = (mib * 1024 * 1024 for mib in (12, 53, 60))
NOTE = 8


def along_bulk(value, steps):
    count = lax.axis_size("bulk")
    leading, last = (max(0, -steps), min(count, count - steps))
    return lax.ppermute(value, "bulk", [(s, s + steps) for s in range(leading, last)])


def trade(value, start):
    count = lax.axis_size("bulk")
    pairs = [(s, s + 1) for s in range(start, count - 1, 2)]
    return lax.ppermute(value, "bulk", pairs + [(b, a) for a, b in pairs])


def from_block(value, offset):
    count = lax.axis_size("contact")
    return lax.ppermute(value, "contact", [((d + offset) % count, d) for d in range(count)])


def everywhere(spread):
    return lax.all_to_all(spread, everyone, 0, 0, tiled=True)


def split(value):
    high = value.astype(bf16)
    return high, (value - high.astype(f32)).astype(bf16)


def mul(left, right, contract=1):
    def one(a, b):
        return lax.dot_general(a, b, (((contract,), (0,)), ((), ())), preferred_element_type=f32)

    return one(left[0], right[0]) + (one(left[0], right[1]) + one(left[1], right[0]))


def col(value):
    return jnp.sum(value, axis=0, keepdims=True)


def place():
    bulk_at = lax.axis_index("bulk")
    own = (bulk_at < lax.axis_size("bulk") - 1).astype(f32)
    prev = (bulk_at > 0).astype(f32)
    return bulk_at % 2 == 0, own, prev


def named(notes):
    here = lax.axis_index("contact").astype(f32)
    return [jnp.where(note[0:1] == here, note[1:2], 0.0) for note in notes]


def push(slave, masters, own, others):
    out = mul(slave, split(own), 0)
    for block, dual in zip(masters, others):
        out = out - mul(block, split(dual), 0)
    return out


def chosen(master_map, blocks):
    count = lax.axis_size("contact")
    offset = lax.rem(master_map[0] - lax.axis_index("contact") + count, count)
    return jnp.where(offset == 1, blocks[0], jnp.where(offset == 2, blocks[1], blocks[2]))


def spread_sums(out, rows):
    n = rows[0].shape[1] // 2
    tile = jnp.concatenate([row[:, i * n : (i + 1) * n] for row in rows for i in range(2)], axis=0)
    out[...] = jnp.broadcast_to(tile[None], out.shape)


def gather_sums(got, k):
    tile = jnp.sum(got[...], axis=0)
    return [jnp.concatenate([tile[2 * i : 2 * i + 1], tile[2 * i + 1 : 2 * i + 2]], axis=1) for i in range(k)]


def kinds_of(step_type, at):
    kind = step_type[at : at + 1]
    return kind == 1, (kind == 0).astype(f32), (kind == 1).astype(f32), (kind == 2).astype(f32)


def direction(kinds, glue, contact, active):
    _, is_cg, is_expand, is_chop = kinds
    keep = is_cg + is_expand
    return (
        [keep * g for g in glue],
        [
            keep * g * (1.0 - a) + is_chop * jnp.minimum(g, 0.0) * a
            for g, a in zip(contact, active)
        ],
    )


def correction(kinds, expand, lam, contact, surfaces):
    return [
        kinds[2] * s * jnp.maximum(expand * d - v, 0.0) for v, d, s in zip(lam, contact, surfaces)
    ]


def base_kernel(k_ref, force_ref, base_ref, high_ref, low_ref):
    step = pl.program_id(0)
    high, low = split(k_ref[...])
    part = mul((high, low), split(force_ref[...]))

    @pl.when(step == 0)
    def _():
        base_ref[...] = part

    @pl.when(step > 0)
    def _():
        base_ref[...] += part

    @pl.when(step < 3)
    def _():
        high_ref[...] = high
        low_ref[...] = low


def prepare_kernel(
    master, lam, slave, active, master_map, on_surface, first_out, second_out, later_out
):
    m, n = lam.shape
    row = lax.broadcasted_iota(jnp.int32, (NOTE, n), 0)
    first_out[2 * m :] = jnp.where(
        row == 0, master_map[0], jnp.where(row == 1, on_surface[0], 0)
    ).astype(f32)
    first_out[:m] = master[...]
    first_out[m : 2 * m] = lam[...]
    first_out.send()
    second_out[:m] = slave[...]
    second_out[m:] = active[0].astype(f32)
    second_out.send()
    later_out[...] = active[1].astype(f32)


def send_faces(y, first_out, second_out, f):
    even, _, _ = place()
    first_out[...] = jnp.where(even, y[f : 2 * f], y[:f])
    second_out[...] = jnp.where(even, y[:f], y[f : 2 * f])
    first_out.send()
    second_out.send()


def glue_gaps(left, right, first_got, second_got):
    even, own, prev = place()
    after = jnp.where(even, first_got, second_got)
    before = jnp.where(even, second_got, first_got)
    return [(right - after) * own, (before - left) * prev]


def faces_of(first_sent, second_sent):
    even, _, _ = place()
    return jnp.where(even, second_sent, first_sent), jnp.where(even, first_sent, second_sent)


def contact_gaps(slaves, masters, own, blocks, master_map, surfaces):
    own_s = split(own)
    block_s = [split(v) for v in blocks]
    picked = tuple(chosen(master_map, [v[i] for v in block_s]) for i in range(2))
    out = [surfaces[0] * (mul(slaves[0], own_s) - mul(masters[0], picked))]
    for o in range(3):
        out.append(surfaces[o + 1] * (mul(slaves[o + 1], block_s[o]) - mul(masters[o + 1], own_s)))
    return out


def unpack(first, first_r, first_l, m_far, note_far):
    m = m_far.shape[0]
    top, rest = pl.ds(0, m), pl.ds(m, m + NOTE)
    masters = (first.part(top), first_r.part(top), m_far, first_l.part(top))
    notes = (first.part(rest), first_r.part(rest), note_far, first_l.part(rest))
    return masters, notes


def start_kernel(
    slave, first, first_r, first_l, m_far, note_far, lam_glue, lam_prev, high, low, base,
    on_surface, first_out, second_out, contact_out,
):
    f = lam_glue.shape[0]
    m = slave.shape[0]
    _, own, _ = place()
    surface = on_surface[0].astype(f32)
    masters, notes = unpack(first, first_r, first_l, m_far, note_far)
    duals = [v[:m] * name for v, name in zip(notes[1:], named([v[m:] for v in notes[1:]]))]
    contact = push(split(slave[...]), Blocks(masters[1:])[:], notes[0][:m] * surface, duals)
    w = jnp.concatenate([-lam_prev[...], lam_glue[...] * own, contact], axis=0)
    y = mul((high[...], low[...]), split(w)) - base[...]
    send_faces(y, first_out, second_out, f)
    contact_out[...] = y[2 * f :]


class Blocks:
    def __init__(self, refs):
        self.refs, self.ready = refs, {}

    def __getitem__(self, at):
        if isinstance(at, slice):
            return [self[i] for i in range(*at.indices(len(self.refs)))]
        if at not in self.ready:
            self.ready[at] = split(self.refs[at][...])
        return self.ready[at]


def first_kernel(
    first_sent, second_sent, contact_sent, first_got, second_got, c1, c2, c3,
    second, second_r, second_l, s_far, a_far, first, first_r, first_l, m_far, note_far,
    step_type, expand_len, high, low, master_map,
    sums_out, first_out, second_out, contact_out, glue_state, contact_state, w_state, y_state, face_out,
):
    f = first_sent.shape[0]
    m = s_far.shape[0]
    mortar, all_notes = unpack(first, first_r, first_l, m_far, note_far)
    top, rest = pl.ds(0, m), pl.ds(m, m)
    slave_refs = (second.part(top), second_r.part(top), s_far, second_l.part(top))
    act_refs = (second.part(rest), second_r.part(rest), a_far, second_l.part(rest))
    surfaces = [v[m:][1:2] for v in all_notes]
    names = named([v[m:] for v in all_notes[1:]])
    slaves, masters = Blocks(slave_refs), Blocks(mortar)
    left, right = faces_of(first_sent[...], second_sent[...])
    glue = glue_gaps(left, right, first_got[...], second_got[...])
    contact = contact_gaps(
        slaves, masters, contact_sent[...], [c1[...], c2[...], c3[...]], master_map, surfaces
    )
    for at, g in enumerate(glue):
        glue_state[at * f : (at + 1) * f] = g
    for at, g in enumerate(contact):
        contact_state[at * m : (at + 1) * m] = g
    glue_state.send()
    contact_state.send()

    kinds = kinds_of(step_type, 0)
    expand = expand_len[...]
    dir_g, dir_c = direction(kinds, glue, contact, [v[...] for v in act_refs])
    fix = correction(kinds, expand, [v[:m] for v in all_notes], dir_c, surfaces)

    w = jnp.concatenate(
        [-dir_g[1], dir_g[0], push(slaves[0], masters[1:], dir_c[0], [d * b for d, b in zip(dir_c[1:], names)])],
        axis=0,
    )
    w_fix = push(slaves[0], masters[1:], fix[0], [d * b for d, b in zip(fix[1:], names)])
    w_state[...] = w
    w_state.send()
    y = mul((high[...], low[...]), split(w))
    y_fix = mul((high[:, 2 * f :], low[:, 2 * f :]), split(w_fix))
    sent = jnp.where(kinds[0], expand * y - y_fix, y)
    send_faces(sent, first_out, second_out, f)
    contact_out[...] = sent[2 * f :]
    contact_out.send()
    face_out[...] = y[2 * f :]
    face_out.send()
    y_state[...] = y
    y_state.send()
    zero = jnp.zeros_like(expand)
    spread_sums(
        sums_out,
        [col(w * y), col(glue[0] * dir_g[0]) + col(contact[0] * dir_c[0]), col(w * y_fix), zero],
    )


def second_kernel(
    contact_sent, c1, c2, c3, first, second, first_r, second_r, note_far, m_far, s_far, first_l,
    second_l, a_far, first_sent, second_sent, first_got, second_got, step_type, expand_len, got, glue_state, contact_state, lam_glue,
    l0, l_r, l_far, l_l, high, low, y_state, w_state, master_map,
    sums_out, left_out, contact_out, right_out, own_out, rows_out,
):
    f = first_sent.shape[0]
    m = s_far.shape[0]
    _, own, _ = place()
    mortar, all_notes = unpack(first, first_r, first_l, m_far, note_far)
    top, rest = pl.ds(0, m), pl.ds(m, m)
    slave_refs = (second.part(top), second_r.part(top), s_far, second_l.part(top))
    act_refs = (second.part(rest), second_r.part(rest), a_far, second_l.part(rest))
    surfaces = [v[m:][1:2] for v in all_notes]
    names = named([v[m:] for v in all_notes[1:]])
    slaves, masters = Blocks(slave_refs), Blocks(mortar)
    image_c = contact_gaps(
        slaves, masters, contact_sent[...], [c1[...], c2[...], c3[...]], master_map, surfaces
    )
    left, right = faces_of(first_sent[...], second_sent[...])
    image_g = glue_gaps(left, right, first_got[...], second_got[...])

    kinds = kinds_of(step_type, 0)
    expand = expand_len[...]
    curv0, desc0, cross0 = gather_sums(got, 3)
    step = jnp.where(kinds[0], expand, desc0 / curv0)
    scale = jnp.where(kinds[0], 1.0, step)
    glue = [glue_state[at * f : (at + 1) * f] for at in range(2)]
    contact = [contact_state[at * m : (at + 1) * m] for at in range(4)]
    lam_c = [v[:m] for v in all_notes]
    dir_g, dir_c = direction(kinds, glue, contact, [v[...] for v in act_refs])
    fix = correction(kinds, expand, lam_c, dir_c, surfaces)
    lam_c = [v - step * d + x for v, d, x in zip(lam_c, dir_c, fix)]
    own_out[0] = lam_glue[...] * own - step * dir_g[0]
    glue = [g - scale * x for g, x in zip(glue, image_g)]
    contact = [g - scale * x for g, x in zip(contact, image_c)]

    kinds = kinds_of(step_type, 1)
    free_g, free_c = direction(
        kinds, glue, contact,
        [l0[...], l_r[...], l_far[...], l_l[...]],
    )
    fix = correction(kinds, expand, lam_c, free_c, surfaces)
    own_out[1] = lam_c[0] + fix[0]
    own_out[2] = glue[0]
    own_out[3] = contact[0]
    own_out[4] = free_g[0]
    own_out[5] = free_c[0]
    own_out[6] = dir_g[0]
    own_out[7] = dir_c[0]
    own_out.send()
    length = jnp.where(kinds[0], expand, 1.0)
    dual = [length * d - x for d, x in zip(free_c, fix)]
    w = jnp.concatenate(
        [
            -length * free_g[1],
            length * free_g[0],
            push(slaves[0], masters[1:], dual[0], [d * b for d, b in zip(dual[1:], names)]),
        ],
        axis=0,
    )
    y = mul((high[...], low[...]), split(w))
    w_dir, y_dir = w_state[...], y_state[...]
    left_out[:f] = y[:f]
    left_out[f:] = y_dir[:f]
    right_out[:f] = y[f : 2 * f]
    right_out[f:] = y_dir[f : 2 * f]
    contact_out[...] = y[2 * f :]
    for out in (left_out, right_out, contact_out):
        out.send()
    first = col(w * y_dir)
    spread_sums(
        sums_out,
        [
            first,
            first + col(w_dir * y),
            col(w * y),
            col(glue[0] * free_g[0]) + col(contact[0] * free_c[0]),
        ],
    )
    left_over = desc0 - step * curv0 + kinds_of(step_type, 0)[2] * cross0
    rows_out[...] = jnp.concatenate([curv0, left_over] + [curv0] * 6, axis=0)


def closing_kernel(
    step_type, expand_len, got, rows, own_in, contact_sent, face_sent, slave, right, on_surface,
    lam_g, lam_c, part_g, part_c, rows_out,
):
    f = right.shape[0] // 2
    _, own, _ = place()
    surface = on_surface[0].astype(f32)
    kinds = kinds_of(step_type, 1)
    expand = expand_len[...]
    first, cross, curv, desc = gather_sums(got, 4)
    curv0, left_over = rows[0:1], rows[1:2]
    conj = jnp.where(step_type[1:2] == 0, first / curv0, 0.0)
    curv = curv - conj * cross + conj * conj * curv0
    desc = desc - conj * left_over
    step = jnp.where(kinds[0], expand, desc / curv)
    scale = jnp.where(kinds[0], 1.0, step)
    lam_g[...] = own_in[0] - step * (own_in[4] - conj * own_in[6])
    lam_c[...] = own_in[1] - step * (own_in[5] - conj * own_in[7])
    lam_g.send()
    lam_c.send()
    part_g[...] = own_in[2] - (scale * own) * (right[:f] - conj * right[f:])
    part_c[...] = own_in[3] - (scale * surface) * mul(
        split(slave[...]), split(contact_sent[...] - conj * face_sent[...])
    )
    rows_out[...] = jnp.concatenate([conj, scale] + [scale] * 6, axis=0)


def last_kernel(
    rows, master, c1, c2, c3, d1, d2, d3, part_c, part_g, after, master_map, on_surface,
    grad_g, grad_c,
):
    f = after.shape[0] // 2
    _, own, _ = place()
    surface = on_surface[0].astype(f32)
    conj, scale = rows[0:1], rows[1:2]
    picked = chosen(master_map, [v[...] for v in (c1, c2, c3)]) - conj * chosen(
        master_map, [v[...] for v in (d1, d2, d3)]
    )
    grad_c[...] = part_c[...] + (scale * surface) * mul(split(master[...]), split(picked))
    grad_c.send()
    grad_g[...] = part_g[...] + (scale * own) * (after[:f] - conj * after[f:])


class Part:
    def __init__(self, whole, index):
        self.whole, self.index = whole, index

    @property
    def shape(self):
        return self.whole.ref.at[self.index].shape

    def __getitem__(self, index):
        return self.whole.arrived().at[self.index][index]


class Operand:
    def __init__(self, source, ref, sem):
        self.ref, self.here = ref, False
        self.copy = pltpu.make_async_copy(source, ref, sem)
        self.copy.start()

    @property
    def shape(self):
        return self.ref.shape

    @property
    def at(self):
        return self

    def arrived(self):
        if not self.here:
            self.copy.wait()
            self.here = True
        return self.ref

    def __getitem__(self, index):
        return self.arrived()[index]

    def part(self, index):
        return Part(self, index)


class Result:
    def __init__(self, target, ref, sem):
        self.ref, self.sent = ref, False
        self.copy = pltpu.make_async_copy(ref, target, sem)

    @property
    def shape(self):
        return self.ref.shape

    def __setitem__(self, index, value):
        self.ref[index] = value

    def send(self):
        if not self.sent:
            self.copy.start()
            self.sent = True


class Held(Operand):
    def __init__(self, ref):
        self.ref, self.here = ref, True


def call(kernel, operands, shapes, scalars=(), near=False, vmem=large_vmem):
    arrays = [] if near else [at for at in range(len(operands)) if at not in scalars]
    n_in, n_out = len(operands), len(shapes)

    def body(*refs):
        given, results, scratch = refs[:n_in], refs[n_in : n_in + n_out], refs[n_in + n_out :]
        sems_in, sems_out = scratch[-2:]
        ins = [v if at in scalars else Held(v) for at, v in enumerate(given)]
        for slot, at in enumerate(arrays):
            ins[at] = Operand(given[at], scratch[slot], sems_in.at[slot])
        outs = [
            Result(results[at], scratch[len(arrays) + at], sems_out.at[at]) for at in range(n_out)
        ]
        kernel(*ins, *outs)
        for at in arrays:
            ins[at].arrived()
        for out in outs:
            out.send()
        for out in outs:
            out.copy.wait()

    return pl.pallas_call(
        body,
        out_shape=[jax.ShapeDtypeStruct(s, f32) for s in shapes],
        in_specs=[
            pl.BlockSpec(
                memory_space=pltpu.SMEM if at in scalars else pltpu.VMEM if near else pltpu.HBM
            )
            for at in range(n_in)
        ],
        out_specs=[pl.BlockSpec(memory_space=pltpu.HBM) for _ in shapes],
        scratch_shapes=[pltpu.VMEM(operands[at].shape, operands[at].dtype) for at in arrays]
        + [pltpu.VMEM(s, f32) for s in shapes]
        + [pltpu.SemaphoreType.DMA((max(1, len(arrays)),)), pltpu.SemaphoreType.DMA((n_out,))],
        compiler_params=pltpu.CompilerParams(vmem_limit_bytes=vmem),
        name=kernel.__name__,
    )(*operands)


def per_device(
    k_inv, mortar_slave, mortar_master, force, lam_glue, lam_contact, master_map, on_surface,
    step_type, active, expand_len,
):
    f, n = lam_glue.shape
    m = lam_contact.shape[0]
    rows = 2 * f + m
    order = k_inv.shape[0]
    block = order // 8
    count = lax.axis_size("bulk") * lax.axis_size("contact")
    face, sums = (f, n), (count, 8, n // 2)
    expand = expand_len[None]

    first, second, later = call(
        prepare_kernel,
        (mortar_master, lam_contact, mortar_slave, active, master_map, on_surface),
        [(2 * m + NOTE, n), (2 * m, n), (m, n)],
        (4, 5),
    )
    first_r, first_l = from_block(first, 1), from_block(first, 3)
    second_r, second_l = from_block(second, 1), from_block(second, 3)
    lam_prev = along_bulk(lam_glue, 1)
    base, high, low = pl.pallas_call(
        base_kernel,
        grid=(8,),
        in_specs=[
            pl.BlockSpec((rows, block), lambda j: (0, j)),
            pl.BlockSpec((block, n), lambda j: (j, 0)),
        ],
        out_specs=[
            pl.BlockSpec((rows, n), lambda j: (0, 0)),
            pl.BlockSpec((rows, block), lambda j: (0, jnp.minimum(j, 2))),
            pl.BlockSpec((rows, block), lambda j: (0, jnp.minimum(j, 2))),
        ],
        out_shape=[
            jax.ShapeDtypeStruct((rows, n), f32),
            jax.ShapeDtypeStruct((rows, rows), bf16),
            jax.ShapeDtypeStruct((rows, rows), bf16),
        ],
        compiler_params=pltpu.CompilerParams(vmem_limit_bytes=small_vmem),
        cost_estimate=pl.CostEstimate(
            flops=12 * rows * order * n, bytes_accessed=4 * order * (rows + n), transcendentals=0
        ),
        name="base_kernel",
    )(k_inv, force)
    first_r, first_l, base = lax.optimization_barrier((first_r, first_l, base))
    m_far, note_far = from_block(first_l[:m], 3), from_block(first_r[m:], 1)
    s_far, a_far = from_block(second_l[:m], 3), from_block(second_r[m:], 1)
    firsts = (first, first_r, first_l, m_far, note_far)
    seconds = (second, second_r, second_l, s_far, a_far)

    def group(value):
        right, left, across = (from_block(value, o) for o in (1, 3, 2))
        return right, across, left

    def exchange(first, second, contact):
        got = trade(first, 0), trade(second, 1)
        return got + group(contact)

    one, two, contact = call(
        start_kernel,
        (mortar_slave, *firsts, lam_glue, lam_prev, high, low, base, on_surface),
        [face, face, (m, n)],
        (11,),
        near=True,
        vmem=small_vmem,
    )
    got = exchange(one, two, contact)
    later, held = lax.optimization_barrier((later, got[1]))
    got = (got[0], held) + got[2:]
    laters = (later,) + group(later)
    spread, one, two, contact, glue_state, contact_state, w_state, y_state, face_dir = call(
        first_kernel,
        (one, two, contact, *got, *seconds, *firsts, step_type, expand, high, low, master_map),
        [sums, face, face, (m, n), (2 * f, n), (4 * m, n), (rows, n), (rows, n), (m, n)],
        (22,),
        near=True,
        vmem=middle_vmem,
    )
    one, two, contact, spread, laters = lax.optimization_barrier((one, two, contact, spread, laters))
    got = exchange(one, two, contact)
    spread, faces = lax.optimization_barrier((spread, got[:2]))
    got = faces + got[2:]
    totals = everywhere(spread)
    face_dir, got = lax.optimization_barrier((face_dir, got))
    dirs = group(face_dir)
    spread, left, contact, right, own, kept = call(
        second_kernel,
        (contact, *got[2:], first, second, first_r, second_r, note_far, m_far, s_far, first_l,
         second_l, a_far, one, two, *got[:2], step_type, expand, totals, glue_state, contact_state, lam_glue, *laters, high, low, y_state, w_state, master_map),
        [sums, (2 * f, n), (m, n), (2 * f, n), (8, f, n), (8, n)],
        (32,),
    )
    left, contact, spread, dirs = lax.optimization_barrier((left, contact, spread, dirs))
    after = along_bulk(left, -1)
    others = group(contact)
    totals = everywhere(spread)
    lam_g, lam_c, part_g, part_c, kept = call(
        closing_kernel,
        (step_type, expand, totals, kept, own, contact, face_dir, mortar_slave, right, on_surface),
        [face, (m, n), face, (m, n), (8, n)],
        (9,),
    )
    grad_g, grad_c = call(
        last_kernel,
        (kept, mortar_master, *others, *dirs, part_c, part_g, after, master_map, on_surface),
        [face, (m, n)],
        (11, 12),
    )
    return lam_g, lam_c, grad_g, grad_c


def solution(mesh):
    whole = P(("bulk", "contact"), None)
    flat = P(("bulk", "contact"))
    return jax.shard_map(
        per_device,
        mesh=mesh,
        in_specs=(
            whole, whole, whole, whole, whole, whole, flat, flat,
            P(), P(None, ("bulk", "contact"), None), P(),
        ),
        out_specs=(whole, whole, whole, whole),
        check_vma=False,
    )
```

```python
import functools

import jax
import jax.numpy as jnp
from jax import lax
from jax.experimental import pallas as pl
from jax.experimental.pallas import tpu as pltpu
from jax.sharding import PartitionSpec as P

everyone = ("bulk", "contact")
f32, bf16 = jnp.float32, jnp.bfloat16
small_vmem, middle_vmem, large_vmem = (mib * 1024 * 1024 for mib in (12, 53, 60))
NOTE = 8


def along_bulk(value, steps):
    count = lax.axis_size("bulk")
    leading, last = (max(0, -steps), min(count, count - steps))
    return lax.ppermute(value, "bulk", [(s, s + steps) for s in range(leading, last)])


def trade(value, start):
    count = lax.axis_size("bulk")
    pairs = [(s, s + 1) for s in range(start, count - 1, 2)]
    return lax.ppermute(value, "bulk", pairs + [(b, a) for a, b in pairs])


def from_block(value, offset):
    count = lax.axis_size("contact")
    return lax.ppermute(value, "contact", [((d + offset) % count, d) for d in range(count)])


def everywhere(spread):
    return lax.all_to_all(spread, everyone, 0, 0, tiled=True)


def split(value):
    high = value.astype(bf16)
    return high, (value - high.astype(f32)).astype(bf16)


def mul(left, right, contract=1):
    def one(a, b):
        return lax.dot_general(a, b, (((contract,), (0,)), ((), ())), preferred_element_type=f32)

    return one(left[0], right[0]) + (one(left[0], right[1]) + one(left[1], right[0]))


def col(value):
    return jnp.sum(value, axis=0, keepdims=True)


def place():
    bulk_at = lax.axis_index("bulk")
    own = (bulk_at < lax.axis_size("bulk") - 1).astype(f32)
    prev = (bulk_at > 0).astype(f32)
    return bulk_at % 2 == 0, own, prev


def named(notes):
    here = lax.axis_index("contact").astype(f32)
    return [jnp.where(note[0:1] == here, note[1:2], 0.0) for note in notes]


def push(slave, masters, own, others):
    out = mul(slave, split(own), 0)
    for block, dual in zip(masters, others):
        out = out - mul(block, split(dual), 0)
    return out


def chosen(master_map, blocks):
    count = lax.axis_size("contact")
    offset = lax.rem(master_map[0] - lax.axis_index("contact") + count, count)
    return jnp.where(offset == 1, blocks[0], jnp.where(offset == 2, blocks[1], blocks[2]))


def spread_sums(out, rows):
    n = rows[0].shape[1] // 2
    tile = jnp.concatenate([row[:, i * n : (i + 1) * n] for row in rows for i in range(2)], axis=0)
    out[...] = jnp.broadcast_to(tile[None], out.shape)


def gather_sums(got, k):
    tile = jnp.sum(got[...], axis=0)
    return [jnp.concatenate([tile[2 * i : 2 * i + 1], tile[2 * i + 1 : 2 * i + 2]], axis=1) for i in range(k)]


def kinds_of(step_type, at):
    kind = step_type[at : at + 1]
    return kind == 1, (kind == 0).astype(f32), (kind == 1).astype(f32), (kind == 2).astype(f32)


def direction(kinds, glue, contact, active):
    _, is_cg, is_expand, is_chop = kinds
    keep = is_cg + is_expand
    return (
        [keep * g for g in glue],
        [
            keep * g * (1.0 - a) + is_chop * jnp.minimum(g, 0.0) * a
            for g, a in zip(contact, active)
        ],
    )


def correction(kinds, expand, lam, contact, surfaces):
    return [
        kinds[2] * s * jnp.maximum(expand * d - v, 0.0) for v, d, s in zip(lam, contact, surfaces)
    ]


def base_kernel(k_ref, force_ref, base_ref, high_ref, low_ref):
    step = pl.program_id(0)
    high, low = split(k_ref[...])
    part = mul((high, low), split(force_ref[...]))

    @pl.when(step == 0)
    def _():
        base_ref[...] = part

    @pl.when(step > 0)
    def _():
        base_ref[...] += part

    @pl.when(step < 3)
    def _():
        high_ref[...] = high
        low_ref[...] = low


def prepare_kernel(
    master, lam, slave, active, master_map, on_surface, first_out, second_out, later_out
):
    m, n = lam.shape
    row = lax.broadcasted_iota(jnp.int32, (NOTE, n), 0)
    first_out[2 * m :] = jnp.where(
        row == 0, master_map[0], jnp.where(row == 1, on_surface[0], 0)
    ).astype(f32)
    first_out[:m] = master[...]
    first_out[m : 2 * m] = lam[...]
    first_out.send()
    second_out[:m] = slave[...]
    second_out[m:] = active[0].astype(f32)
    second_out.send()
    later_out[...] = active[1].astype(f32)


def send_faces(y, first_out, second_out, f):
    even, _, _ = place()
    first_out[...] = jnp.where(even, y[f : 2 * f], y[:f])
    second_out[...] = jnp.where(even, y[:f], y[f : 2 * f])
    first_out.send()
    second_out.send()


def glue_gaps(left, right, first_got, second_got):
    even, own, prev = place()
    after = jnp.where(even, first_got, second_got)
    before = jnp.where(even, second_got, first_got)
    return [(right - after) * own, (before - left) * prev]


def faces_of(first_sent, second_sent):
    even, _, _ = place()
    return jnp.where(even, second_sent, first_sent), jnp.where(even, first_sent, second_sent)


def contact_gaps(slaves, masters, own, blocks, master_map, surfaces):
    own_s = split(own)
    block_s = [split(v) for v in blocks]
    picked = tuple(chosen(master_map, [v[i] for v in block_s]) for i in range(2))
    out = [surfaces[0] * (mul(slaves[0], own_s) - mul(masters[0], picked))]
    for o in range(3):
        out.append(surfaces[o + 1] * (mul(slaves[o + 1], block_s[o]) - mul(masters[o + 1], own_s)))
    return out


def unpack(first, first_r, first_l, m_far, note_far):
    m = m_far.shape[0]
    top, rest = pl.ds(0, m), pl.ds(m, m + NOTE)
    masters = (first.part(top), first_r.part(top), m_far, first_l.part(top))
    notes = (first.part(rest), first_r.part(rest), note_far, first_l.part(rest))
    return masters, notes


def start_kernel(
    slave, first, first_r, first_l, m_far, note_far, lam_glue, lam_prev, high, low, base,
    on_surface, first_out, second_out, contact_out,
):
    f = lam_glue.shape[0]
    m = slave.shape[0]
    _, own, _ = place()
    surface = on_surface[0].astype(f32)
    masters, notes = unpack(first, first_r, first_l, m_far, note_far)
    duals = [v[:m] * name for v, name in zip(notes[1:], named([v[m:] for v in notes[1:]]))]
    contact = push(split(slave[...]), Blocks(masters[1:])[:], notes[0][:m] * surface, duals)
    w = jnp.concatenate([-lam_prev[...], lam_glue[...] * own, contact], axis=0)
    y = mul((high[...], low[...]), split(w)) - base[...]
    send_faces(y, first_out, second_out, f)
    contact_out[...] = y[2 * f :]


class Blocks:
    def __init__(self, refs):
        self.refs, self.ready = refs, {}

    def __getitem__(self, at):
        if isinstance(at, slice):
            return [self[i] for i in range(*at.indices(len(self.refs)))]
        if at not in self.ready:
            self.ready[at] = split(self.refs[at][...])
        return self.ready[at]


def first_kernel(
    first_sent, second_sent, contact_sent, first_got, second_got, c1, c2, c3,
    second, second_r, second_l, s_far, a_far, first, first_r, first_l, m_far, note_far,
    step_type, expand_len, high, low, master_map,
    sums_out, first_out, second_out, contact_out, glue_state, contact_state, w_state, y_state, face_out,
):
    f = first_sent.shape[0]
    m = s_far.shape[0]
    mortar, all_notes = unpack(first, first_r, first_l, m_far, note_far)
    top, rest = pl.ds(0, m), pl.ds(m, m)
    slave_refs = (second.part(top), second_r.part(top), s_far, second_l.part(top))
    act_refs = (second.part(rest), second_r.part(rest), a_far, second_l.part(rest))
    surfaces = [v[m:][1:2] for v in all_notes]
    names = named([v[m:] for v in all_notes[1:]])
    slaves, masters = Blocks(slave_refs), Blocks(mortar)
    left, right = faces_of(first_sent[...], second_sent[...])
    glue = glue_gaps(left, right, first_got[...], second_got[...])
    contact = contact_gaps(
        slaves, masters, contact_sent[...], [c1[...], c2[...], c3[...]], master_map, surfaces
    )
    for at, g in enumerate(glue):
        glue_state[at * f : (at + 1) * f] = g
    for at, g in enumerate(contact):
        contact_state[at * m : (at + 1) * m] = g
    glue_state.send()
    contact_state.send()

    kinds = kinds_of(step_type, 0)
    expand = expand_len[...]
    dir_g, dir_c = direction(kinds, glue, contact, [v[...] for v in act_refs])
    fix = correction(kinds, expand, [v[:m] for v in all_notes], dir_c, surfaces)

    w = jnp.concatenate(
        [-dir_g[1], dir_g[0], push(slaves[0], masters[1:], dir_c[0], [d * b for d, b in zip(dir_c[1:], names)])],
        axis=0,
    )
    w_fix = push(slaves[0], masters[1:], fix[0], [d * b for d, b in zip(fix[1:], names)])
    w_state[...] = w[2 * f :]
    w_state.send()
    y = mul((high[...], low[...]), split(w))
    y_fix = mul((high[:, 2 * f :], low[:, 2 * f :]), split(w_fix))
    sent = jnp.where(kinds[0], expand * y - y_fix, y)
    send_faces(sent, first_out, second_out, f)
    contact_out[...] = sent[2 * f :]
    contact_out.send()
    face_out[...] = y[2 * f :]
    face_out.send()
    y_state[...] = y[: 2 * f]
    y_state.send()
    zero = jnp.zeros_like(expand)
    spread_sums(
        sums_out,
        [col(w * y), col(glue[0] * dir_g[0]) + col(contact[0] * dir_c[0]), col(w * y_fix), zero],
    )


def second_kernel(
    contact_sent, c1, c2, c3, first, second, first_r, second_r, note_far, m_far, s_far, first_l,
    second_l, a_far, first_sent, second_sent, first_got, second_got, step_type, expand_len, got, glue_state, contact_state, lam_glue,
    l0, l_r, l_far, l_l, high, low, y_state, face_state, w_state, master_map,
    sums_out, left_out, contact_out, right_out, own_out, rows_out,
):
    f = first_sent.shape[0]
    m = s_far.shape[0]
    _, own, _ = place()
    mortar, all_notes = unpack(first, first_r, first_l, m_far, note_far)
    top, rest = pl.ds(0, m), pl.ds(m, m)
    slave_refs = (second.part(top), second_r.part(top), s_far, second_l.part(top))
    act_refs = (second.part(rest), second_r.part(rest), a_far, second_l.part(rest))
    surfaces = [v[m:][1:2] for v in all_notes]
    names = named([v[m:] for v in all_notes[1:]])
    slaves, masters = Blocks(slave_refs), Blocks(mortar)
    image_c = contact_gaps(
        slaves, masters, contact_sent[...], [c1[...], c2[...], c3[...]], master_map, surfaces
    )
    left, right = faces_of(first_sent[...], second_sent[...])
    image_g = glue_gaps(left, right, first_got[...], second_got[...])

    kinds = kinds_of(step_type, 0)
    expand = expand_len[...]
    curv0, desc0, cross0 = gather_sums(got, 3)
    step = jnp.where(kinds[0], expand, desc0 / curv0)
    scale = jnp.where(kinds[0], 1.0, step)
    glue = [glue_state[at * f : (at + 1) * f] for at in range(2)]
    contact = [contact_state[at * m : (at + 1) * m] for at in range(4)]
    lam_c = [v[:m] for v in all_notes]
    dir_g, dir_c = direction(kinds, glue, contact, [v[...] for v in act_refs])
    fix = correction(kinds, expand, lam_c, dir_c, surfaces)
    lam_c = [v - step * d + x for v, d, x in zip(lam_c, dir_c, fix)]
    own_out[0] = lam_glue[...] * own - step * dir_g[0]
    glue = [g - scale * x for g, x in zip(glue, image_g)]
    contact = [g - scale * x for g, x in zip(contact, image_c)]

    kinds = kinds_of(step_type, 1)
    free_g, free_c = direction(
        kinds, glue, contact,
        [l0[...], l_r[...], l_far[...], l_l[...]],
    )
    fix = correction(kinds, expand, lam_c, free_c, surfaces)
    own_out[1] = lam_c[0] + fix[0]
    own_out[2] = glue[0]
    own_out[3] = contact[0]
    own_out[4] = free_g[0]
    own_out[5] = free_c[0]
    own_out[6] = dir_g[0]
    own_out[7] = dir_c[0]
    own_out.send()
    length = jnp.where(kinds[0], expand, 1.0)
    dual = [length * d - x for d, x in zip(free_c, fix)]
    w = jnp.concatenate(
        [
            -length * free_g[1],
            length * free_g[0],
            push(slaves[0], masters[1:], dual[0], [d * b for d, b in zip(dual[1:], names)]),
        ],
        axis=0,
    )
    y = mul((high[...], low[...]), split(w))
    w_dir = jnp.concatenate([-dir_g[1], dir_g[0], w_state[...]], axis=0)
    y_dir = jnp.concatenate([y_state[...], face_state[...]], axis=0)
    left_out[:f] = y[:f]
    left_out[f:] = y_dir[:f]
    right_out[:f] = y[f : 2 * f]
    right_out[f:] = y_dir[f : 2 * f]
    contact_out[...] = y[2 * f :]
    for out in (left_out, right_out, contact_out):
        out.send()
    first = col(w * y_dir)
    spread_sums(
        sums_out,
        [
            first,
            first + col(w_dir * y),
            col(w * y),
            col(glue[0] * free_g[0]) + col(contact[0] * free_c[0]),
        ],
    )
    left_over = desc0 - step * curv0 + kinds_of(step_type, 0)[2] * cross0
    rows_out[...] = jnp.concatenate([curv0, left_over] + [curv0] * 6, axis=0)


def closing_kernel(
    step_type, expand_len, got, rows, own_in, contact_sent, face_sent, slave, right, on_surface,
    lam_g, lam_c, part_g, part_c, rows_out,
):
    f = right.shape[0] // 2
    _, own, _ = place()
    surface = on_surface[0].astype(f32)
    kinds = kinds_of(step_type, 1)
    expand = expand_len[...]
    first, cross, curv, desc = gather_sums(got, 4)
    curv0, left_over = rows[0:1], rows[1:2]
    conj = jnp.where(step_type[1:2] == 0, first / curv0, 0.0)
    curv = curv - conj * cross + conj * conj * curv0
    desc = desc - conj * left_over
    step = jnp.where(kinds[0], expand, desc / curv)
    scale = jnp.where(kinds[0], 1.0, step)
    lam_g[...] = own_in[0] - step * (own_in[4] - conj * own_in[6])
    lam_c[...] = own_in[1] - step * (own_in[5] - conj * own_in[7])
    lam_g.send()
    lam_c.send()
    part_g[...] = own_in[2] - (scale * own) * (right[:f] - conj * right[f:])
    part_c[...] = own_in[3] - (scale * surface) * mul(
        split(slave[...]), split(contact_sent[...] - conj * face_sent[...])
    )
    rows_out[...] = jnp.concatenate([conj, scale] + [scale] * 6, axis=0)


def last_kernel(
    rows, master, c1, c2, c3, d1, d2, d3, part_c, part_g, after, master_map, on_surface,
    grad_g, grad_c,
):
    f = after.shape[0] // 2
    _, own, _ = place()
    surface = on_surface[0].astype(f32)
    conj, scale = rows[0:1], rows[1:2]
    picked = chosen(master_map, [v[...] for v in (c1, c2, c3)]) - conj * chosen(
        master_map, [v[...] for v in (d1, d2, d3)]
    )
    grad_c[...] = part_c[...] + (scale * surface) * mul(split(master[...]), split(picked))
    grad_c.send()
    grad_g[...] = part_g[...] + (scale * own) * (after[:f] - conj * after[f:])


class Part:
    def __init__(self, whole, index):
        self.whole, self.index = whole, index

    @property
    def shape(self):
        return self.whole.ref.at[self.index].shape

    def __getitem__(self, index):
        return self.whole.arrived().at[self.index][index]


class Operand:
    def __init__(self, source, ref, sem):
        self.ref, self.here = ref, False
        self.copy = pltpu.make_async_copy(source, ref, sem)
        self.copy.start()

    @property
    def shape(self):
        return self.ref.shape

    @property
    def at(self):
        return self

    def arrived(self):
        if not self.here:
            self.copy.wait()
            self.here = True
        return self.ref

    def __getitem__(self, index):
        return self.arrived()[index]

    def part(self, index):
        return Part(self, index)


class Result:
    def __init__(self, target, ref, sem):
        self.ref, self.sent = ref, False
        self.copy = pltpu.make_async_copy(ref, target, sem)

    @property
    def shape(self):
        return self.ref.shape

    def __setitem__(self, index, value):
        self.ref[index] = value

    def send(self):
        if not self.sent:
            self.copy.start()
            self.sent = True


class Held(Operand):
    def __init__(self, ref):
        self.ref, self.here = ref, True


def call(kernel, operands, shapes, scalars=(), near=False, vmem=large_vmem):
    arrays = [] if near else [at for at in range(len(operands)) if at not in scalars]
    n_in, n_out = len(operands), len(shapes)

    def body(*refs):
        given, results, scratch = refs[:n_in], refs[n_in : n_in + n_out], refs[n_in + n_out :]
        sems_in, sems_out = scratch[-2:]
        ins = [v if at in scalars else Held(v) for at, v in enumerate(given)]
        for slot, at in enumerate(arrays):
            ins[at] = Operand(given[at], scratch[slot], sems_in.at[slot])
        outs = [
            Result(results[at], scratch[len(arrays) + at], sems_out.at[at]) for at in range(n_out)
        ]
        kernel(*ins, *outs)
        for at in arrays:
            ins[at].arrived()
        for out in outs:
            out.send()
        for out in outs:
            out.copy.wait()

    return pl.pallas_call(
        body,
        out_shape=[jax.ShapeDtypeStruct(s, f32) for s in shapes],
        in_specs=[
            pl.BlockSpec(
                memory_space=pltpu.SMEM if at in scalars else pltpu.VMEM if near else pltpu.HBM
            )
            for at in range(n_in)
        ],
        out_specs=[pl.BlockSpec(memory_space=pltpu.HBM) for _ in shapes],
        scratch_shapes=[pltpu.VMEM(operands[at].shape, operands[at].dtype) for at in arrays]
        + [pltpu.VMEM(s, f32) for s in shapes]
        + [pltpu.SemaphoreType.DMA((max(1, len(arrays)),)), pltpu.SemaphoreType.DMA((n_out,))],
        compiler_params=pltpu.CompilerParams(vmem_limit_bytes=vmem),
        name=kernel.__name__,
    )(*operands)


def per_device(
    k_inv, mortar_slave, mortar_master, force, lam_glue, lam_contact, master_map, on_surface,
    step_type, active, expand_len,
):
    f, n = lam_glue.shape
    m = lam_contact.shape[0]
    rows = 2 * f + m
    order = k_inv.shape[0]
    block = order // 8
    count = lax.axis_size("bulk") * lax.axis_size("contact")
    face, sums = (f, n), (count, 8, n // 2)
    expand = expand_len[None]

    first, second, later = call(
        prepare_kernel,
        (mortar_master, lam_contact, mortar_slave, active, master_map, on_surface),
        [(2 * m + NOTE, n), (2 * m, n), (m, n)],
        (4, 5),
    )
    first_r, first_l = from_block(first, 1), from_block(first, 3)
    second_r, second_l = from_block(second, 1), from_block(second, 3)
    lam_prev = along_bulk(lam_glue, 1)
    base, high, low = pl.pallas_call(
        base_kernel,
        grid=(8,),
        in_specs=[
            pl.BlockSpec((rows, block), lambda j: (0, j)),
            pl.BlockSpec((block, n), lambda j: (j, 0)),
        ],
        out_specs=[
            pl.BlockSpec((rows, n), lambda j: (0, 0)),
            pl.BlockSpec((rows, block), lambda j: (0, jnp.minimum(j, 2))),
            pl.BlockSpec((rows, block), lambda j: (0, jnp.minimum(j, 2))),
        ],
        out_shape=[
            jax.ShapeDtypeStruct((rows, n), f32),
            jax.ShapeDtypeStruct((rows, rows), bf16),
            jax.ShapeDtypeStruct((rows, rows), bf16),
        ],
        compiler_params=pltpu.CompilerParams(vmem_limit_bytes=small_vmem),
        cost_estimate=pl.CostEstimate(
            flops=12 * rows * order * n, bytes_accessed=4 * order * (rows + n), transcendentals=0
        ),
        name="base_kernel",
    )(k_inv, force)
    first_r, first_l, base = lax.optimization_barrier((first_r, first_l, base))
    m_far, note_far = from_block(first_l[:m], 3), from_block(first_r[m:], 1)
    s_far, a_far = from_block(second_l[:m], 3), from_block(second_r[m:], 1)
    firsts = (first, first_r, first_l, m_far, note_far)
    seconds = (second, second_r, second_l, s_far, a_far)

    def group(value):
        right, left, across = (from_block(value, o) for o in (1, 3, 2))
        return right, across, left

    def exchange(first, second, contact):
        got = trade(first, 0), trade(second, 1)
        return got + group(contact)

    one, two, contact = call(
        start_kernel,
        (mortar_slave, *firsts, lam_glue, lam_prev, high, low, base, on_surface),
        [face, face, (m, n)],
        (11,),
        near=True,
        vmem=small_vmem,
    )
    got = exchange(one, two, contact)
    later, got = lax.optimization_barrier((later, got))
    laters = (later,) + group(later)
    spread, one, two, contact, glue_state, contact_state, w_state, y_state, face_dir = call(
        first_kernel,
        (one, two, contact, *got, *seconds, *firsts, step_type, expand, high, low, master_map),
        [sums, face, face, (m, n), (2 * f, n), (4 * m, n), (m, n), (2 * f, n), (m, n)],
        (22,),
        near=True,
        vmem=middle_vmem,
    )
    one, two, contact, spread, laters = lax.optimization_barrier((one, two, contact, spread, laters))
    got = exchange(one, two, contact)
    spread, faces = lax.optimization_barrier((spread, got[:2]))
    got = faces + got[2:]
    totals = everywhere(spread)
    face_dir, got = lax.optimization_barrier((face_dir, got))
    dirs = group(face_dir)
    spread, left, contact, right, own, kept = call(
        second_kernel,
        (contact, *got[2:], first, second, first_r, second_r, note_far, m_far, s_far, first_l,
         second_l, a_far, one, two, *got[:2], step_type, expand, totals, glue_state, contact_state, lam_glue, *laters, high, low, y_state, face_dir,
         w_state, master_map),
        [sums, (2 * f, n), (m, n), (2 * f, n), (8, f, n), (8, n)],
        (33,),
    )
    left, contact, spread, dirs = lax.optimization_barrier((left, contact, spread, dirs))
    after = along_bulk(left, -1)
    others = group(contact)
    totals = everywhere(spread)
    lam_g, lam_c, part_g, part_c, kept = call(
        closing_kernel,
        (step_type, expand, totals, kept, own, contact, face_dir, mortar_slave, right, on_surface),
        [face, (m, n), face, (m, n), (8, n)],
        (9,),
    )
    grad_g, grad_c = call(
        last_kernel,
        (kept, mortar_master, *others, *dirs, part_c, part_g, after, master_map, on_surface),
        [face, (m, n)],
        (11, 12),
    )
    return lam_g, lam_c, grad_g, grad_c


def solution(mesh):
    whole = P(("bulk", "contact"), None)
    flat = P(("bulk", "contact"))
    return jax.shard_map(
        per_device,
        mesh=mesh,
        in_specs=(
            whole, whole, whole, whole, whole, whole, flat, flat,
            P(), P(None, ("bulk", "contact"), None), P(),
        ),
        out_specs=(whole, whole, whole, whole),
        check_vma=False,
    )
```
